32 devices in a mesh: date: 8 (over z, x), space: 4 (over y, core).
Axes of the slice: x: 2, y: 2, z: 4, core: 2. Of those that a mesh axis runs over, the one named last changes fastest.
Arguments:
- frames: bfloat16 [32, 1024, 1024], P('date', 'space'), may hold values from -6 to 6
- cloud_mask: int32 [32, 1024], P('date', 'space'), may hold values from 0 to 1
- qkv_weight: bfloat16 [2, 1024, 3072], replicated, may hold values from -0.1875 to 0.1875
- out_weight: bfloat16 [2, 1024, 1024], replicated, may hold values from -0.1875 to 0.1875
- norm_gain: float32 [2, 1024], replicated, may hold values from 0.1 to 1.9
- head_norm_scale: float32 [2, 1024], replicated, may hold values from 0.1 to 1.9
- decay: float32 [2, 32, 16], P(None, 'date'), as said below
Outputs:
- forecast: bfloat16 [32, 1024, 1024], P('date', 'space')
The draws below stay inside these ranges and needn't reach their ends.
Inputs may be any that keep to these rules, and one draw needn't show every extreme that they name: `decay`: every entry lies strictly between 0 and 1.
All inputs are finite; a program needn't handle non-finite values.
Results may differ from the reference program's by a relative error of at most 0.0065.
Values may be sent and summed in bfloat16 or wider, within the bound.
A program may use at most 128 MiB of HBM per device.

```python
import jax
import jax.numpy as jnp
from jax import lax

D = 1024
HEADS = 16
HEAD = 64
STACK_LEVELS = 2
DATE_DEV = 4
TIME_POINTS = 32
SPACE = 1024


def draw_decay(key, part):
    lookup_vectors = jax.random.split(key, 6)
    share = 0.5
    picker = jax.random.uniform(lookup_vectors[0], (STACK_LEVELS, 1, HEADS))
    slow = (picker < share) & (picker > jnp.min(picker, axis=2, keepdims=True))
    reach = jax.random.uniform(lookup_vectors[1], (STACK_LEVELS, 1, HEADS), minval=0.2, maxval=0.9)
    slow_rate = jnp.exp(-jnp.log(10.0) * reach / TIME_POINTS)
    fast_rate = jax.random.uniform(lookup_vectors[2], (STACK_LEVELS, 1, HEADS), minval=0.4, maxval=0.7)
    jitter = jax.random.uniform(lookup_vectors[3], (STACK_LEVELS, TIME_POINTS, HEADS), minval=0.97, maxval=1.0)
    recent_span = jax.random.uniform(lookup_vectors[4], (STACK_LEVELS, TIME_POINTS, 1)) < jnp.minimum(1.0, 3.0 / TIME_POINTS)
    level_index = jax.random.uniform(lookup_vectors[5], (STACK_LEVELS, TIME_POINTS, 1), minval=0.5, maxval=0.8)
    fading_rate = jnp.where(slow, slow_rate, fast_rate) * jitter
    fading_rate = jnp.where(recent_span, fading_rate * level_index, fading_rate)
    return fading_rate.astype(jnp.float32)


def draw_cloud_mask(key, part):
    streams = jax.random.split(jax.random.fold_in(key, 71), 3)
    tiles = jax.random.randint(streams[0], (TIME_POINTS, SPACE), 0, 4) < 3
    seasons = max(1, TIME_POINTS // 32)
    season_length = jax.random.randint(streams[1], (seasons,), 3 * DATE_DEV, 4 * DATE_DEV)
    season_start = jax.random.randint(streams[2], (seasons,), DATE_DEV, TIME_POINTS - 4 * DATE_DEV + 2)
    dates = jnp.arange(TIME_POINTS, dtype=jnp.int32)[:, None]
    inside = (dates >= season_start[None, :]) & (dates < season_start[None, :] + season_length[None, :])
    overcast = jnp.any(inside, axis=1)
    return jnp.where(overcast[:, None], 0, tiles.astype(jnp.int32)).astype(jnp.int32)


def block_scale(own_key, extent, shards, smallest, top_value):
    def one(position, blocks):
        heights = jax.random.uniform(jax.random.fold_in(jax.random.fold_in(own_key, 6), position), (blocks,), jnp.float32, smallest / len(shards), top_value / len(shards))
        return jnp.repeat(jnp.exp(heights), extent[position] // blocks).reshape((-1,) + (1,) * (len(extent) - position - 1))

    level = one(*shards[0])
    for cut in shards[1:]:
        level = level * one(*cut)
    return level


def normal_values(key, dims, scale, bound, pieces=(), kind=jnp.bfloat16):
    level = block_scale(key, dims, pieces, -0.22, 0.18) if pieces else 1.0
    array = jax.random.normal(key, dims, jnp.float32) * scale * level
    return jnp.minimum(jnp.maximum(array, -bound), bound).astype(kind)


def setup_inputs(seed: int = 0) -> dict:
    seeds = jax.random.split(jax.random.key(seed), 8)
    return {
        "frames": normal_values(seeds[0], (TIME_POINTS, SPACE, D), 1.0, 6.0, ((0, 8), (1, 4))),
        "cloud_mask": draw_cloud_mask(jax.random.fold_in(seeds[7], 71), 0),
        "qkv_weight": normal_values(seeds[2], (STACK_LEVELS, D, 3 * D), D ** -0.5, 0.1875),
        "out_weight": normal_values(seeds[3], (STACK_LEVELS, D, D), D ** -0.5, 0.1875),
        "norm_gain": jnp.clip(1.0 + 0.18 * jax.random.normal(seeds[4], (STACK_LEVELS, D), jnp.float32), 0.1, 1.9),
        "head_norm_scale": jnp.clip(1.0 + 0.18 * jax.random.normal(seeds[5], (STACK_LEVELS, D), jnp.float32), 0.1, 1.9),
        "decay": draw_decay(jax.random.fold_in(seeds[7], 71), 0),
    }


def feature(u):
    return jax.nn.elu(u) + 1.0

def one_layer(frames, cloud_mask, w_qkv, w_out, gain, h_gain, decay_l):

    def step(state, inputs):
        tokens, flags, persist_factor = inputs
        xf = tokens.astype(jnp.float32)
        in_msq = lax.optimization_barrier(jnp.mean(xf * xf, -1, keepdims=True)) + 1e-05
        normalized_output = (xf * lax.rsqrt(in_msq) * gain).astype(jnp.bfloat16)
        proj = jnp.dot(normalized_output, w_qkv, preferred_element_type=jnp.float32)
        flag_f = flags.astype(jnp.float32)[:, None]
        query = feature(proj[:, :D]).astype(jnp.bfloat16).reshape(-1, HEADS, HEAD)
        key = (feature(proj[:, D:2 * D]) * flag_f).astype(jnp.bfloat16).reshape(-1, HEADS, HEAD)
        value = proj[:, 2 * D:].astype(jnp.bfloat16).reshape(-1, HEADS, HEAD)
        kv = jnp.einsum('she,shf->hef', key.astype(jnp.float32), value.astype(jnp.float32))
        state = persist_factor[:, None, None] * state + kv
        state_b = state.astype(jnp.bfloat16)
        numer = jnp.einsum('she,hef->shf', query.astype(jnp.float32), state_b.astype(jnp.float32))
        head_msq = lax.optimization_barrier(jnp.mean(numer * numer, -1, keepdims=True)) + 1e-05
        numer = numer * lax.rsqrt(head_msq)
        mixed = (numer.reshape(-1, D) * h_gain).astype(jnp.bfloat16)
        result = (xf + jnp.dot(mixed, w_out, preferred_element_type=jnp.float32)).astype(jnp.bfloat16)
        return (state, result)
    start = jnp.zeros((HEADS, HEAD, HEAD), jnp.float32)
    _, result = lax.scan(step, start, (frames, cloud_mask, decay_l))
    return result

def reference(frames, cloud_mask, qkv_weight, out_weight, norm_gain, head_norm_scale, decay):
    current = frames
    for layer in range(STACK_LEVELS):
        current = one_layer(current, cloud_mask, qkv_weight[layer], out_weight[layer], norm_gain[layer], head_norm_scale[layer], decay[layer])
    return current
```

```python
import functools

import jax
import jax.numpy as jnp
from jax import lax
from jax.experimental import pallas as pl
from jax.experimental.pallas import tpu as pltpu
from jax.sharding import PartitionSpec as P

HEADS = 16
HEAD = 64
LAYERS = 2
COLS = 256
MESH = pl.DeviceIdType.MESH


def feature(u):
    return jnp.where(u > 0.0, u + 1.0, jnp.exp(jnp.minimum(u, 0.0)))


def kernel(
    shards, spans, dates,
    frames, mask, wqkv, wout, gain, hscale, tbl, out,
    wbuf, nb, qb, mb, maskb, kb, vb, part, lst, rs_send, rs_recv, dsend, drecv, sb, tks,
    fsem, wsem, rs_ss, rs_rs, d_ss, d_rs, ag_ss, ag_rs, tk_ss, tk_rs,
):
    tokens, width = out.shape
    here = tokens // dates
    groups = width // COLS
    rows = HEAD // shards
    me_s, me_d = lax.axis_index("space"), lax.axis_index("date")

    def peer(off):
        return lax.rem(me_s + off, shards)

    barrier = pltpu.get_barrier_semaphore()
    for off in range(1, shards):
        pl.semaphore_signal(barrier, inc=1, device_id={"space": peer(off)}, device_id_type=MESH)
    for off in range(1, spans):
        pl.semaphore_signal(
            barrier, inc=1, device_id={"date": lax.rem(me_d + off, spans)}, device_id_type=MESH
        )

    def frame_copy():
        return pltpu.make_async_copy(frames, out, fsem)

    def qkv_copy(l, c):
        cols = pl.ds(pl.multiple_of(c * COLS, COLS), COLS)
        return pltpu.make_async_copy(wqkv.at[l, :, cols], wbuf.at[l, c], wsem.at[l, c])

    def out_copy(l, c):
        cols = pl.ds(pl.multiple_of(c * COLS, COLS), COLS)
        slot = c + 3 * groups
        return pltpu.make_async_copy(wout.at[l, :, cols], wbuf.at[l, slot], wsem.at[l, slot])

    frame_copy().start()
    for l in range(LAYERS):
        for g in range(groups):
            qkv_copy(l, groups + g).start()
            qkv_copy(l, 2 * groups + g).start()
        for g in range(groups):
            qkv_copy(l, g).start()
        for g in range(groups):
            out_copy(l, g).start()

    flags = mask[...].astype(jnp.float32)
    for t in range(dates):
        pick = lax.broadcasted_iota(jnp.int32, (dates, COLS), 0) == t
        maskb[pl.ds(t * here, here), :] = lax.dot_general(
            flags, jnp.where(pick, 1.0, 0.0), (((0,), (0,)), ((), ())),
            preferred_element_type=jnp.float32,
        )

    pl.semaphore_wait(barrier, shards + spans - 2)

    def tk_copy(j):
        return pltpu.make_async_remote_copy(
            src_ref=tbl.at[8:16], dst_ref=tks.at[me_d], send_sem=tk_ss.at[j],
            recv_sem=tk_rs.at[me_d], device_id={"date": j}, device_id_type=MESH,
        )

    def tk_arrival(j):
        return pltpu.make_async_remote_copy(
            src_ref=tbl.at[8:16], dst_ref=tks.at[j], send_sem=tk_ss.at[j],
            recv_sem=tk_rs.at[j], device_id={"date": j}, device_id_type=MESH,
        )

    def rs_copy(l, g, p, slot):
        return pltpu.make_async_remote_copy(
            src_ref=rs_send.at[l, g, p], dst_ref=rs_recv.at[l, g, slot],
            send_sem=rs_ss.at[l, g, p], recv_sem=rs_rs.at[l, g, slot],
            device_id={"space": p}, device_id_type=MESH,
        )

    def d_copy(l, g, j, slot):
        return pltpu.make_async_remote_copy(
            src_ref=dsend.at[l, g], dst_ref=drecv.at[l, g, slot],
            send_sem=d_ss.at[l, g, j], recv_sem=d_rs.at[l, g, slot],
            device_id={"date": j}, device_id_type=MESH,
        )

    def ag_copy(l, g, p, slot):
        return pltpu.make_async_remote_copy(
            src_ref=sb.at[l, g, slot], dst_ref=sb.at[l, g, slot],
            send_sem=ag_ss.at[l, g, p], recv_sem=ag_rs.at[l, g, slot],
            device_id={"space": p}, device_id_type=MESH,
        )

    def later(f):
        def body(j, c):
            f(j)
            return c

        lax.fori_loop(me_d + 1, spans, body, 0)

    later(lambda j: tk_copy(j).start())
    frame_copy().wait()

    def columns(g):
        return pl.ds(pl.multiple_of(g * COLS, COLS), COLS)

    def by_layer(ref, l, first, second, cols):
        return jnp.where(l == 0, ref[first : first + 1, cols], ref[second : second + 1, cols])

    def norm(l):
        scale = jnp.where(l == 0, gain[0:1, :], gain[1:2, :])

        def body(t, c):
            at = pl.ds(pl.multiple_of(t * 64, 64), 64)
            xf = out[at, :].astype(jnp.float32)
            msq = jnp.mean(xf * xf, -1, keepdims=True) + 1e-05
            nb[at, :] = (xf * lax.rsqrt(msq) * scale).astype(jnp.bfloat16)
            return c

        lax.fori_loop(0, tokens // 64, body, 0)

    def keys(l, g):
        qkv_copy(l, groups + g).wait()
        qkv_copy(l, 2 * groups + g).wait()
        k = jnp.dot(nb[...], wbuf[l, groups + g], preferred_element_type=jnp.float32)
        kb[...] = (feature(k) * maskb[...]).astype(jnp.bfloat16)
        vb[...] = jnp.dot(
            nb[...], wbuf[l, 2 * groups + g], preferred_element_type=jnp.float32
        ).astype(jnp.bfloat16)
        head = lax.broadcasted_iota(jnp.int32, (HEAD, COLS), 1) // HEAD
        for t in range(dates):
            at = pl.ds(t * here, here)
            pair = lax.dot_general(
                kb[at, :], vb[at, :], (((0,), (0,)), ((), ())), preferred_element_type=jnp.float32
            )
            small = jnp.zeros((HEAD, COLS), jnp.float32)
            for h in range(COLS // HEAD):
                small = jnp.where(head == h, pair[h * HEAD : (h + 1) * HEAD, :], small)
            for r in range(shards):
                part[g, r, pl.ds(t * rows, rows), :] = small[r * rows : (r + 1) * rows, :]
        for r in range(shards):
            rs_send[l, g, r] = part[g, r].astype(jnp.bfloat16)
        for off in range(1, shards):
            rs_copy(l, g, peer(off), me_s).start()

    def queries(l, g):
        qkv_copy(l, g).wait()
        q = jnp.dot(nb[...], wbuf[l, g], preferred_element_type=jnp.float32)
        qb[g] = feature(q).astype(jnp.bfloat16)

    def decays(l, g, t):
        return by_layer(tbl, l, t, dates + t, columns(g))

    def summed(l, g):
        total = part[g, me_s]
        for off in range(1, shards):
            p = peer(off)
            rs_copy(l, g, p, p).wait_recv()
            total = total + rs_recv[l, g, p].astype(jnp.float32)
        state = jnp.zeros((rows, COLS), jnp.float32)
        for t in range(dates):
            state = decays(l, g, t) * state + total[t * rows : (t + 1) * rows, :]
            lst[g, pl.ds(t * rows, rows), :] = state
        dsend[l, g] = state.astype(dsend.dtype)
        later(lambda j: d_copy(l, g, j, me_d).start())

    def joined(l, g):
        @pl.when((l == 0) & (g == 0))
        def _():
            def arrive(j, c):
                tk_arrival(j).wait_recv()
                return c

            lax.fori_loop(0, me_d, arrive, 0)

        def earlier(j, carry):
            d_copy(l, g, j, j).wait_recv()
            kept = jnp.where(l == 0, tks[j, 0:1, columns(g)], tks[j, 1:2, columns(g)])
            return kept * carry + drecv[l, g, j].astype(jnp.float32)

        carry = lax.fori_loop(0, me_d, earlier, jnp.zeros((rows, COLS), jnp.float32))
        states = []
        for t in range(dates):
            carry = decays(l, g, t) * carry
            states.append(lst[g, pl.ds(t * rows, rows), :] + carry)
        sb[l, g, me_s] = jnp.concatenate(states, 0).astype(jnp.bfloat16)
        for off in range(1, shards):
            ag_copy(l, g, peer(off), me_s).start()

    def mix(l, g):
        for off in range(1, shards):
            p = peer(off)
            ag_copy(l, g, p, p).wait_recv()
        blocks = [sb[l, g, r].astype(jnp.float32) for r in range(shards)]
        head = lax.broadcasted_iota(jnp.int32, (HEAD, COLS), 1) // HEAD
        wide = lax.broadcasted_iota(jnp.int32, (COLS, COLS), 1) // HEAD
        tall = lax.broadcasted_iota(jnp.int32, (COLS, COLS), 0) // HEAD
        ones = jnp.where(wide == tall, 1.0, 0.0).astype(jnp.bfloat16)
        scale = by_layer(hscale, l, 0, 1, columns(g))
        for t in range(dates):
            small = jnp.concatenate([b[t * rows : (t + 1) * rows, :] for b in blocks], 0)
            big = jnp.concatenate(
                [jnp.where(head == h, small, 0.0) for h in range(COLS // HEAD)], 0
            ).astype(jnp.bfloat16)
            numer = jnp.dot(
                qb[g, pl.ds(t * here, here), :], big, preferred_element_type=jnp.float32
            )
            msq = jnp.dot(
                (numer * numer).astype(jnp.bfloat16), ones, preferred_element_type=jnp.float32
            )
            msq = msq * (1.0 / HEAD) + 1e-05
            mb[pl.ds(t * here, here), columns(g)] = (numer * lax.rsqrt(msq) * scale).astype(
                jnp.bfloat16
            )

    def project(l, c):
        out_copy(l, c).wait()
        update = jnp.dot(mb[...], wbuf[l, 3 * groups + c], preferred_element_type=jnp.float32)
        at = columns(c)
        out[:, at] = (out[:, at].astype(jnp.float32) + update).astype(jnp.bfloat16)

    def layer(l, c0):
        norm(l)

        def step(s, c):
            @pl.when(s < groups)
            def _():
                keys(l, s)

            @pl.when(s >= groups)
            def _():
                queries(l, s - groups)

            @pl.when((s >= 1) & (s < groups + 1))
            def _():
                summed(l, s - 1)

            @pl.when((s >= 3) & (s < groups + 3))
            def _():
                joined(l, s - 3)

            return c

        lax.fori_loop(0, 2 * groups, step, 0)

        def mix_step(g, c):
            mix(l, g)
            return c

        lax.fori_loop(0, groups, mix_step, 0)

        def project_step(g, c):
            project(l, g)
            return c

        lax.fori_loop(0, groups, project_step, 0)
        return c0

    lax.fori_loop(0, LAYERS, layer, 0)

    later(lambda j: tk_copy(j).wait_send())

    def drain(i, c):
        l, g = i // groups, lax.rem(i, groups)
        for off in range(1, shards):
            rs_copy(l, g, peer(off), me_s).wait_send()
            ag_copy(l, g, peer(off), me_s).wait_send()
        later(lambda j: d_copy(l, g, j, me_d).wait_send())
        return c

    lax.fori_loop(0, LAYERS * groups, drain, 0)


def local(shards, spans, frames, cloud_mask, qkv_weight, out_weight, norm_gain, head_norm_scale, decay):
    dates, here, width = frames.shape
    tokens = dates * here
    groups = width // COLS
    rows = HEAD // shards
    wire = jnp.bfloat16 if rows % 16 == 0 else jnp.float32
    wide = jnp.repeat(decay, HEAD, axis=2)
    kept = jnp.prod(wide, axis=1)
    tbl = jnp.concatenate(
        [wide.reshape(LAYERS * dates, width), kept, jnp.zeros((6, width), jnp.float32)], 0
    )
    vmem = pl.BlockSpec(memory_space=pltpu.VMEM)
    hbm = pl.BlockSpec(memory_space=pl.ANY)
    bf16, f32 = jnp.bfloat16, jnp.float32
    block = (shards, dates * rows, COLS)
    dma = pltpu.SemaphoreType.DMA
    out = pl.pallas_call(
        functools.partial(kernel, shards, spans, dates),
        out_shape=jax.ShapeDtypeStruct((tokens, width), bf16),
        in_specs=[hbm, vmem, hbm, hbm, vmem, vmem, vmem],
        out_specs=vmem,
        scratch_shapes=[
            pltpu.VMEM((LAYERS, 4 * groups, width, COLS), bf16),
            pltpu.VMEM((tokens, width), bf16),
            pltpu.VMEM((groups, tokens, COLS), bf16),
            pltpu.VMEM((tokens, width), bf16),
            pltpu.VMEM((tokens, COLS), f32),
            pltpu.VMEM((tokens, COLS), bf16),
            pltpu.VMEM((tokens, COLS), bf16),
            pltpu.VMEM((groups,) + block, f32),
            pltpu.VMEM((groups, dates * rows, COLS), f32),
            pltpu.VMEM((LAYERS, groups) + block, bf16),
            pltpu.VMEM((LAYERS, groups) + block, bf16),
            pltpu.VMEM((LAYERS, groups, rows, COLS), wire),
            pltpu.VMEM((LAYERS, groups, spans, rows, COLS), wire),
            pltpu.VMEM((LAYERS, groups) + block, bf16),
            pltpu.VMEM((spans, 8, width), f32),
            dma,
            dma((LAYERS, 4 * groups)),
            dma((LAYERS, groups, shards)),
            dma((LAYERS, groups, shards)),
            dma((LAYERS, groups, spans)),
            dma((LAYERS, groups, spans)),
            dma((LAYERS, groups, shards)),
            dma((LAYERS, groups, shards)),
            dma((spans,)),
            dma((spans,)),
        ],
        compiler_params=pltpu.CompilerParams(
            collective_id=0, has_side_effects=True, vmem_limit_bytes=56 * 2**20
        ),
    )(
        frames.reshape(tokens, width), cloud_mask, qkv_weight, out_weight,
        norm_gain, head_norm_scale, tbl,
    )
    return out.reshape(frames.shape)


def solution(mesh):
    placed = (
        P("date", "space", None),
        P("date", "space"),
        P(),
        P(),
        P(),
        P(),
        P(None, "date", None),
    )
    return jax.shard_map(
        functools.partial(local, mesh.shape["space"], mesh.shape["date"]),
        mesh=mesh,
        in_specs=placed,
        out_specs=P("date", "space", None),
        check_vma=False,
    )
```

```python
import functools

import jax
import jax.numpy as jnp
from jax import lax
from jax.experimental import pallas as pl
from jax.experimental.pallas import tpu as pltpu
from jax.sharding import PartitionSpec as P

HEADS = 16
HEAD = 64
LAYERS = 2
COLS = 256
PIECES = 8
MESH = pl.DeviceIdType.MESH


def feature(u):
    return jnp.where(u > 0.0, u + 1.0, jnp.exp(jnp.minimum(u, 0.0)))


def kernel(
    shards, spans, dates,
    frames, mask, wqkv, wout, gain, hscale, decay, out,
    tbl, wbuf, nb, qb, mb, maskb, kb, vb, part, lst, rs_send, rs_recv, dsend, drecv, sb, tks,
    fsem, wsem, rs_ss, rs_rs, d_ss, d_rs, ag_ss, ag_rs, tk_ss, tk_rs,
):
    tokens, width = out.shape
    here = tokens // dates
    groups = width // COLS
    rows = HEAD // shards
    me_s, me_d = lax.axis_index("space"), lax.axis_index("date")

    def peer(off):
        return lax.rem(me_s + off, shards)

    barrier = pltpu.get_barrier_semaphore()
    for off in range(1, shards):
        pl.semaphore_signal(barrier, inc=1, device_id={"space": peer(off)}, device_id_type=MESH)
    for off in range(1, spans):
        pl.semaphore_signal(
            barrier, inc=1, device_id={"date": lax.rem(me_d + off, spans)}, device_id_type=MESH
        )

    def frame_copy():
        return pltpu.make_async_copy(frames, out, fsem)

    def qkv_copy(l, c):
        cols = pl.ds(pl.multiple_of(c * COLS, COLS), COLS)
        return pltpu.make_async_copy(wqkv.at[l, :, cols], wbuf.at[l, c], wsem.at[l, c])

    def out_copy(l, c):
        cols = pl.ds(pl.multiple_of(c * COLS, COLS), COLS)
        slot = c + 3 * groups
        return pltpu.make_async_copy(wout.at[l, :, cols], wbuf.at[l, slot], wsem.at[l, slot])

    frame_copy().start()
    for l in range(LAYERS):
        for g in range(groups):
            qkv_copy(l, groups + g).start()
            qkv_copy(l, 2 * groups + g).start()
        for g in range(groups):
            qkv_copy(l, g).start()
        for g in range(groups):
            out_copy(l, g).start()

    flags = mask[...].astype(jnp.float32)
    for t in range(dates):
        pick = lax.broadcasted_iota(jnp.int32, (dates, COLS), 0) == t
        maskb[pl.ds(t * here, here), :] = lax.dot_general(
            flags, jnp.where(pick, 1.0, 0.0), (((0,), (0,)), ((), ())),
            preferred_element_type=jnp.float32,
        )

    spread = jnp.where(
        lax.broadcasted_iota(jnp.int32, (HEADS, width), 1) // HEAD
        == lax.broadcasted_iota(jnp.int32, (HEADS, width), 0), 1.0, 0.0,
    )
    tail = []
    for l in range(LAYERS):
        kept_l = jnp.dot(
            decay[l], spread, precision=lax.Precision.HIGHEST, preferred_element_type=jnp.float32
        )
        tbl[pl.ds(l * dates, dates), :] = kept_l
        whole = kept_l[0:1, :]
        for t in range(1, dates):
            whole = whole * kept_l[t : t + 1, :]
        tail.append(whole)
    tbl[8:16, :] = jnp.concatenate(tail + [jnp.zeros((8 - LAYERS, width), jnp.float32)], 0)

    pl.semaphore_wait(barrier, shards + spans - 2)

    def tk_copy(j):
        return pltpu.make_async_remote_copy(
            src_ref=tbl.at[8:16], dst_ref=tks.at[me_d], send_sem=tk_ss.at[j],
            recv_sem=tk_rs.at[me_d], device_id={"date": j}, device_id_type=MESH,
        )

    def tk_arrival(j):
        return pltpu.make_async_remote_copy(
            src_ref=tbl.at[8:16], dst_ref=tks.at[j], send_sem=tk_ss.at[j],
            recv_sem=tk_rs.at[j], device_id={"date": j}, device_id_type=MESH,
        )

    def rs_copy(l, g, p, slot):
        return pltpu.make_async_remote_copy(
            src_ref=rs_send.at[l, g, p], dst_ref=rs_recv.at[l, g, slot],
            send_sem=rs_ss.at[l, g, p], recv_sem=rs_rs.at[l, g, slot],
            device_id={"space": p}, device_id_type=MESH,
        )

    def d_copy(l, g, j, slot):
        return pltpu.make_async_remote_copy(
            src_ref=dsend.at[l, g], dst_ref=drecv.at[l, g, slot],
            send_sem=d_ss.at[l, g, j], recv_sem=d_rs.at[l, g, slot],
            device_id={"date": j}, device_id_type=MESH,
        )

    def ag_copy(l, g, p, slot):
        return pltpu.make_async_remote_copy(
            src_ref=sb.at[l, g, slot], dst_ref=sb.at[l, g, slot],
            send_sem=ag_ss.at[l, g, p], recv_sem=ag_rs.at[l, g, slot],
            device_id={"space": p}, device_id_type=MESH,
        )

    def later(f):
        def body(j, c):
            f(j)
            return c

        lax.fori_loop(me_d + 1, spans, body, 0)

    later(lambda j: tk_copy(j).start())
    frame_copy().wait()

    def columns(g):
        return pl.ds(pl.multiple_of(g * COLS, COLS), COLS)

    def by_layer(ref, l, first, second, cols):
        return jnp.where(l == 0, ref[first : first + 1, cols], ref[second : second + 1, cols])

    def norm(l):
        scale = jnp.where(l == 0, gain[0:1, :], gain[1:2, :])

        def body(t, c):
            at = pl.ds(pl.multiple_of(t * COLS, COLS), COLS)
            xf = out[at, :].astype(jnp.float32)
            msq = jnp.mean(xf * xf, -1, keepdims=True) + 1e-05
            nb[at, :] = (xf * lax.rsqrt(msq) * scale).astype(jnp.bfloat16)
            return c

        lax.fori_loop(0, tokens // COLS, body, 0)

    def keys(l, g):
        qkv_copy(l, groups + g).wait()
        qkv_copy(l, 2 * groups + g).wait()
        k = jnp.dot(nb[...], wbuf[l, groups + g], preferred_element_type=jnp.float32)
        kb[...] = (feature(k) * maskb[...]).astype(jnp.bfloat16)
        vb[...] = jnp.dot(
            nb[...], wbuf[l, 2 * groups + g], preferred_element_type=jnp.float32
        ).astype(jnp.bfloat16)
        head = lax.broadcasted_iota(jnp.int32, (HEAD, COLS), 1) // HEAD
        for t in range(dates):
            at = pl.ds(t * here, here)
            pair = lax.dot_general(
                kb[at, :], vb[at, :], (((0,), (0,)), ((), ())), preferred_element_type=jnp.float32
            )
            small = jnp.zeros((HEAD, COLS), jnp.float32)
            for h in range(COLS // HEAD):
                small = jnp.where(head == h, pair[h * HEAD : (h + 1) * HEAD, :], small)
            for r in range(shards):
                part[g, r, pl.ds(t * rows, rows), :] = small[r * rows : (r + 1) * rows, :]
        for r in range(shards):
            rs_send[l, g, r] = part[g, r].astype(jnp.bfloat16)
        for off in range(1, shards):
            rs_copy(l, g, peer(off), me_s).start()

    def queries(l, g):
        qkv_copy(l, g).wait()
        q = jnp.dot(nb[...], wbuf[l, g], preferred_element_type=jnp.float32)
        qb[g] = feature(q).astype(jnp.bfloat16)

    def decays(l, g, t):
        return by_layer(tbl, l, t, dates + t, columns(g))

    def summed(l, g):
        total = part[g, me_s]
        for off in range(1, shards):
            p = peer(off)
            rs_copy(l, g, p, p).wait_recv()
            total = total + rs_recv[l, g, p].astype(jnp.float32)
        state = jnp.zeros((rows, COLS), jnp.float32)
        for t in range(dates):
            state = decays(l, g, t) * state + total[t * rows : (t + 1) * rows, :]
            lst[g, pl.ds(t * rows, rows), :] = state
        dsend[l, g] = state.astype(dsend.dtype)
        later(lambda j: d_copy(l, g, j, me_d).start())

    def joined(l, g):
        @pl.when((l == 0) & (g == 0))
        def _():
            def arrive(j, c):
                tk_arrival(j).wait_recv()
                return c

            lax.fori_loop(0, me_d, arrive, 0)

        def earlier(j, carry):
            d_copy(l, g, j, j).wait_recv()
            kept = jnp.where(l == 0, tks[j, 0:1, columns(g)], tks[j, 1:2, columns(g)])
            return kept * carry + drecv[l, g, j].astype(jnp.float32)

        carry = lax.fori_loop(0, me_d, earlier, jnp.zeros((rows, COLS), jnp.float32))
        states = []
        for t in range(dates):
            carry = decays(l, g, t) * carry
            states.append(lst[g, pl.ds(t * rows, rows), :] + carry)
        sb[l, g, me_s] = jnp.concatenate(states, 0).astype(jnp.bfloat16)
        for off in range(1, shards):
            ag_copy(l, g, peer(off), me_s).start()

    def mix(l, g):
        for off in range(1, shards):
            p = peer(off)
            ag_copy(l, g, p, p).wait_recv()
        blocks = [sb[l, g, r].astype(jnp.float32) for r in range(shards)]
        head = lax.broadcasted_iota(jnp.int32, (HEAD, COLS), 1) // HEAD
        wide = lax.broadcasted_iota(jnp.int32, (COLS, COLS), 1) // HEAD
        tall = lax.broadcasted_iota(jnp.int32, (COLS, COLS), 0) // HEAD
        ones = jnp.where(wide == tall, 1.0, 0.0).astype(jnp.bfloat16)
        scale = by_layer(hscale, l, 0, 1, columns(g))
        for t in range(dates):
            small = jnp.concatenate([b[t * rows : (t + 1) * rows, :] for b in blocks], 0)
            big = jnp.concatenate(
                [jnp.where(head == h, small, 0.0) for h in range(COLS // HEAD)], 0
            ).astype(jnp.bfloat16)
            numer = jnp.dot(
                qb[g, pl.ds(t * here, here), :], big, preferred_element_type=jnp.float32
            )
            msq = jnp.dot(
                (numer * numer).astype(jnp.bfloat16), ones, preferred_element_type=jnp.float32
            )
            msq = msq * (1.0 / HEAD) + 1e-05
            mb[pl.ds(t * here, here), columns(g)] = (numer * lax.rsqrt(msq) * scale).astype(
                jnp.bfloat16
            )

    def project(l, c):
        out_copy(l, c).wait()
        update = jnp.dot(mb[...], wbuf[l, 3 * groups + c], preferred_element_type=jnp.float32)
        at = columns(c)
        out[:, at] = (out[:, at].astype(jnp.float32) + update).astype(jnp.bfloat16)

    def layer(l, c0):
        norm(l)

        def step(s, c):
            @pl.when(s < groups)
            def _():
                keys(l, s)

            @pl.when(s >= groups)
            def _():
                queries(l, s - groups)

            @pl.when((s >= 2) & (s < groups + 2))
            def _():
                summed(l, s - 2)

            @pl.when(s >= groups)
            def _():
                joined(l, s - groups)

            return c

        lax.fori_loop(0, 2 * groups, step, 0)

        def mix_step(g, c):
            mix(l, g)
            return c

        lax.fori_loop(0, groups, mix_step, 0)

        def project_step(g, c):
            project(l, g)
            return c

        lax.fori_loop(0, groups, project_step, 0)
        return c0

    lax.fori_loop(0, LAYERS, layer, 0)

    later(lambda j: tk_copy(j).wait_send())

    def drain(i, c):
        l, g = i // groups, lax.rem(i, groups)
        for off in range(1, shards):
            rs_copy(l, g, peer(off), me_s).wait_send()
            ag_copy(l, g, peer(off), me_s).wait_send()
        later(lambda j: d_copy(l, g, j, me_d).wait_send())
        return c

    lax.fori_loop(0, LAYERS * groups, drain, 0)


def hand_over(src, dst, sems):
    step = src.shape[0] // PIECES
    copies = [
        pltpu.make_async_copy(src.at[pl.ds(i * step, step)], dst.at[pl.ds(i * step, step)], sems.at[i])
        for i in range(PIECES)
    ]
    for copy in copies:
        copy.start()
    for copy in copies:
        copy.wait()


def local(shards, spans, frames, cloud_mask, qkv_weight, out_weight, norm_gain, head_norm_scale, decay):
    dates, here, width = frames.shape
    tokens = dates * here
    groups = width // COLS
    rows = HEAD // shards
    wire = jnp.bfloat16 if rows % 16 == 0 else jnp.float32
    vmem = pl.BlockSpec(memory_space=pltpu.VMEM)
    hbm = pl.BlockSpec(memory_space=pl.ANY)
    bf16, f32 = jnp.bfloat16, jnp.float32
    block = (shards, dates * rows, COLS)
    dma = pltpu.SemaphoreType.DMA
    out = pl.pallas_call(
        functools.partial(kernel, shards, spans, dates),
        out_shape=jax.ShapeDtypeStruct((tokens, width), bf16),
        in_specs=[hbm, vmem, hbm, hbm, vmem, vmem, vmem],
        out_specs=vmem,
        scratch_shapes=[
            pltpu.VMEM((16, width), f32),
            pltpu.VMEM((LAYERS, 4 * groups, width, COLS), bf16),
            pltpu.VMEM((tokens, width), bf16),
            pltpu.VMEM((groups, tokens, COLS), bf16),
            pltpu.VMEM((tokens, width), bf16),
            pltpu.VMEM((tokens, COLS), f32),
            pltpu.VMEM((tokens, COLS), bf16),
            pltpu.VMEM((tokens, COLS), bf16),
            pltpu.VMEM((groups,) + block, f32),
            pltpu.VMEM((groups, dates * rows, COLS), f32),
            pltpu.VMEM((LAYERS, groups) + block, bf16),
            pltpu.VMEM((LAYERS, groups) + block, bf16),
            pltpu.VMEM((LAYERS, groups, rows, COLS), wire),
            pltpu.VMEM((LAYERS, groups, spans, rows, COLS), wire),
            pltpu.VMEM((LAYERS, groups) + block, bf16),
            pltpu.VMEM((spans, 8, width), f32),
            dma,
            dma((LAYERS, 4 * groups)),
            dma((LAYERS, groups, shards)),
            dma((LAYERS, groups, shards)),
            dma((LAYERS, groups, spans)),
            dma((LAYERS, groups, spans)),
            dma((LAYERS, groups, shards)),
            dma((LAYERS, groups, shards)),
            dma((spans,)),
            dma((spans,)),
        ],
        compiler_params=pltpu.CompilerParams(
            collective_id=0, has_side_effects=True, vmem_limit_bytes=56 * 2**20
        ),
    )(
        frames.reshape(tokens, width), cloud_mask, qkv_weight, out_weight,
        norm_gain, head_norm_scale, decay,
    )
    result = pl.pallas_call(
        hand_over,
        out_shape=jax.ShapeDtypeStruct((tokens, width), bf16),
        in_specs=[hbm],
        out_specs=hbm,
        scratch_shapes=[dma((PIECES,))],
    )(out)
    return result.reshape(frames.shape)


def solution(mesh):
    placed = (
        P("date", "space", None),
        P("date", "space"),
        P(),
        P(),
        P(),
        P(),
        P(None, "date", None),
    )
    return jax.shard_map(
        functools.partial(local, mesh.shape["space"], mesh.shape["date"]),
        mesh=mesh,
        in_specs=placed,
        out_specs=P("date", "space", None),
        check_vma=False,
    )
```

```python
import functools

import jax
import jax.numpy as jnp
from jax import lax
from jax.experimental import pallas as pl
from jax.experimental.pallas import tpu as pltpu
from jax.sharding import PartitionSpec as P

HEADS = 16
HEAD = 64
LAYERS = 2
COLS = 256
MESH = pl.DeviceIdType.MESH


def feature(u):
    return jnp.where(u > 0.0, u + 1.0, jnp.exp(jnp.minimum(u, 0.0)))


def kernel(
    shards, spans, dates,
    frames, mask, wqkv, wout, gain, hscale, decay, out,
    tbl, wbuf, nb, qb, mb, maskb, kb, vb, part, lst, rs_send, rs_recv, dsend, drecv, sb, tks,
    fsem, wsem, rs_ss, rs_rs, d_ss, d_rs, ag_ss, ag_rs, tk_ss, tk_rs,
):
    tokens, width = out.shape
    here = tokens // dates
    groups = width // COLS
    rows = HEAD // shards
    me_s, me_d = lax.axis_index("space"), lax.axis_index("date")

    def peer(off):
        return lax.rem(me_s + off, shards)

    barrier = pltpu.get_barrier_semaphore()
    for off in range(1, shards):
        pl.semaphore_signal(barrier, inc=1, device_id={"space": peer(off)}, device_id_type=MESH)
    for off in range(1, spans):
        pl.semaphore_signal(
            barrier, inc=1, device_id={"date": lax.rem(me_d + off, spans)}, device_id_type=MESH
        )

    def frame_copy():
        return pltpu.make_async_copy(frames, out, fsem)

    def qkv_copy(l, c):
        cols = pl.ds(pl.multiple_of(c * COLS, COLS), COLS)
        return pltpu.make_async_copy(wqkv.at[l, :, cols], wbuf.at[l, c], wsem.at[l, c])

    def out_copy(l, c):
        cols = pl.ds(pl.multiple_of(c * COLS, COLS), COLS)
        slot = c + 3 * groups
        return pltpu.make_async_copy(wout.at[l, :, cols], wbuf.at[l, slot], wsem.at[l, slot])

    frame_copy().start()
    for l in range(LAYERS):
        for g in range(groups):
            qkv_copy(l, groups + g).start()
            qkv_copy(l, 2 * groups + g).start()
        for g in range(groups):
            qkv_copy(l, g).start()
        for g in range(groups):
            out_copy(l, g).start()

    flags = mask[...].astype(jnp.float32)
    for t in range(dates):
        pick = lax.broadcasted_iota(jnp.int32, (dates, COLS), 0) == t
        maskb[pl.ds(t * here, here), :] = lax.dot_general(
            flags, jnp.where(pick, 1.0, 0.0), (((0,), (0,)), ((), ())),
            preferred_element_type=jnp.float32,
        )

    spread = jnp.where(
        lax.broadcasted_iota(jnp.int32, (HEADS, width), 1) // HEAD
        == lax.broadcasted_iota(jnp.int32, (HEADS, width), 0), 1.0, 0.0,
    )
    tail = []
    for l in range(LAYERS):
        kept_l = jnp.dot(
            decay[l], spread, precision=lax.Precision.HIGHEST, preferred_element_type=jnp.float32
        )
        tbl[pl.ds(l * dates, dates), :] = kept_l
        whole = kept_l[0:1, :]
        for t in range(1, dates):
            whole = whole * kept_l[t : t + 1, :]
        tail.append(whole)
    tbl[8:16, :] = jnp.concatenate(tail + [jnp.zeros((8 - LAYERS, width), jnp.float32)], 0)

    pl.semaphore_wait(barrier, shards + spans - 2)

    def tk_copy(j):
        return pltpu.make_async_remote_copy(
            src_ref=tbl.at[8:16], dst_ref=tks.at[me_d], send_sem=tk_ss.at[j],
            recv_sem=tk_rs.at[me_d], device_id={"date": j}, device_id_type=MESH,
        )

    def tk_arrival(j):
        return pltpu.make_async_remote_copy(
            src_ref=tbl.at[8:16], dst_ref=tks.at[j], send_sem=tk_ss.at[j],
            recv_sem=tk_rs.at[j], device_id={"date": j}, device_id_type=MESH,
        )

    def rs_copy(l, g, p, slot):
        return pltpu.make_async_remote_copy(
            src_ref=rs_send.at[l, g, p], dst_ref=rs_recv.at[l, g, slot],
            send_sem=rs_ss.at[l, g, p], recv_sem=rs_rs.at[l, g, slot],
            device_id={"space": p}, device_id_type=MESH,
        )

    def d_copy(l, g, j, slot):
        return pltpu.make_async_remote_copy(
            src_ref=dsend.at[l, g], dst_ref=drecv.at[l, g, slot],
            send_sem=d_ss.at[l, g, j], recv_sem=d_rs.at[l, g, slot],
            device_id={"date": j}, device_id_type=MESH,
        )

    def ag_copy(l, g, p, slot):
        return pltpu.make_async_remote_copy(
            src_ref=sb.at[l, g, slot], dst_ref=sb.at[l, g, slot],
            send_sem=ag_ss.at[l, g, p], recv_sem=ag_rs.at[l, g, slot],
            device_id={"space": p}, device_id_type=MESH,
        )

    def later(f):
        def body(j, c):
            f(j)
            return c

        lax.fori_loop(me_d + 1, spans, body, 0)

    later(lambda j: tk_copy(j).start())
    frame_copy().wait()

    def columns(g):
        return pl.ds(pl.multiple_of(g * COLS, COLS), COLS)

    def by_layer(ref, l, first, second, cols):
        return jnp.where(l == 0, ref[first : first + 1, cols], ref[second : second + 1, cols])

    def norm(l):
        scale = jnp.where(l == 0, gain[0:1, :], gain[1:2, :])

        def body(t, c):
            at = pl.ds(pl.multiple_of(t * COLS, COLS), COLS)
            xf = out[at, :].astype(jnp.float32)
            msq = jnp.mean(xf * xf, -1, keepdims=True) + 1e-05
            nb[at, :] = (xf * lax.rsqrt(msq) * scale).astype(jnp.bfloat16)
            return c

        lax.fori_loop(0, tokens // COLS, body, 0)

    def keys(l, g):
        qkv_copy(l, groups + g).wait()
        qkv_copy(l, 2 * groups + g).wait()
        k = jnp.dot(nb[...], wbuf[l, groups + g], preferred_element_type=jnp.float32)
        kb[...] = (feature(k) * maskb[...]).astype(jnp.bfloat16)
        vb[...] = jnp.dot(
            nb[...], wbuf[l, 2 * groups + g], preferred_element_type=jnp.float32
        ).astype(jnp.bfloat16)
        head = lax.broadcasted_iota(jnp.int32, (HEAD, COLS), 1) // HEAD
        for t in range(dates):
            at = pl.ds(t * here, here)
            pair = lax.dot_general(
                kb[at, :], vb[at, :], (((0,), (0,)), ((), ())), preferred_element_type=jnp.float32
            )
            small = jnp.zeros((HEAD, COLS), jnp.float32)
            for h in range(COLS // HEAD):
                small = jnp.where(head == h, pair[h * HEAD : (h + 1) * HEAD, :], small)
            for r in range(shards):
                part[g, r, pl.ds(t * rows, rows), :] = small[r * rows : (r + 1) * rows, :]
        for r in range(shards):
            rs_send[l, g, r] = part[g, r].astype(jnp.bfloat16)
        for off in range(1, shards):
            rs_copy(l, g, peer(off), me_s).start()

    def queries(l, g):
        qkv_copy(l, g).wait()
        q = jnp.dot(nb[...], wbuf[l, g], preferred_element_type=jnp.float32)
        qb[g] = feature(q).astype(jnp.bfloat16)

    def decays(l, g, t):
        return by_layer(tbl, l, t, dates + t, columns(g))

    def summed(l, g):
        total = part[g, me_s]
        for off in range(1, shards):
            p = peer(off)
            rs_copy(l, g, p, p).wait_recv()
            total = total + rs_recv[l, g, p].astype(jnp.float32)
        state = jnp.zeros((rows, COLS), jnp.float32)
        for t in range(dates):
            state = decays(l, g, t) * state + total[t * rows : (t + 1) * rows, :]
            lst[g, pl.ds(t * rows, rows), :] = state
        dsend[l, g] = state.astype(dsend.dtype)
        later(lambda j: d_copy(l, g, j, me_d).start())

    def joined(l, g):
        @pl.when((l == 0) & (g == 0))
        def _():
            def arrive(j, c):
                tk_arrival(j).wait_recv()
                return c

            lax.fori_loop(0, me_d, arrive, 0)

        def earlier(j, carry):
            d_copy(l, g, j, j).wait_recv()
            kept = jnp.where(l == 0, tks[j, 0:1, columns(g)], tks[j, 1:2, columns(g)])
            return kept * carry + drecv[l, g, j].astype(jnp.float32)

        carry = lax.fori_loop(0, me_d, earlier, jnp.zeros((rows, COLS), jnp.float32))
        states = []
        for t in range(dates):
            carry = decays(l, g, t) * carry
            states.append(lst[g, pl.ds(t * rows, rows), :] + carry)
        sb[l, g, me_s] = jnp.concatenate(states, 0).astype(jnp.bfloat16)
        for off in range(1, shards):
            ag_copy(l, g, peer(off), me_s).start()

    def mix(l, g):
        for off in range(1, shards):
            p = peer(off)
            ag_copy(l, g, p, p).wait_recv()
        blocks = [sb[l, g, r].astype(jnp.float32) for r in range(shards)]
        head = lax.broadcasted_iota(jnp.int32, (HEAD, COLS), 1) // HEAD
        wide = lax.broadcasted_iota(jnp.int32, (COLS, COLS), 1) // HEAD
        tall = lax.broadcasted_iota(jnp.int32, (COLS, COLS), 0) // HEAD
        ones = jnp.where(wide == tall, 1.0, 0.0).astype(jnp.bfloat16)
        scale = by_layer(hscale, l, 0, 1, columns(g))
        for t in range(dates):
            small = jnp.concatenate([b[t * rows : (t + 1) * rows, :] for b in blocks], 0)
            big = jnp.concatenate(
                [jnp.where(head == h, small, 0.0) for h in range(COLS // HEAD)], 0
            ).astype(jnp.bfloat16)
            numer = jnp.dot(
                qb[g, pl.ds(t * here, here), :], big, preferred_element_type=jnp.float32
            )
            msq = jnp.dot(
                (numer * numer).astype(jnp.bfloat16), ones, preferred_element_type=jnp.float32
            )
            msq = msq * (1.0 / HEAD) + 1e-05
            mb[pl.ds(t * here, here), columns(g)] = (numer * lax.rsqrt(msq) * scale).astype(
                jnp.bfloat16
            )

    def project(l, c):
        out_copy(l, c).wait()
        update = jnp.dot(mb[...], wbuf[l, 3 * groups + c], preferred_element_type=jnp.float32)
        at = columns(c)
        out[:, at] = (out[:, at].astype(jnp.float32) + update).astype(jnp.bfloat16)

    def layer(l, c0):
        norm(l)

        def step(s, c):
            @pl.when(s < groups)
            def _():
                keys(l, s)

            @pl.when(s >= groups)
            def _():
                queries(l, s - groups)

            @pl.when((s >= 2) & (s < groups + 2))
            def _():
                summed(l, s - 2)

            @pl.when(s >= groups)
            def _():
                joined(l, s - groups)

            return c

        lax.fori_loop(0, 2 * groups, step, 0)

        def mix_step(g, c):
            mix(l, g)
            return c

        lax.fori_loop(0, groups, mix_step, 0)

        def project_step(g, c):
            project(l, g)
            return c

        lax.fori_loop(0, groups, project_step, 0)
        return c0

    lax.fori_loop(0, LAYERS, layer, 0)

    later(lambda j: tk_copy(j).wait_send())

    def drain(i, c):
        l, g = i // groups, lax.rem(i, groups)
        for off in range(1, shards):
            rs_copy(l, g, peer(off), me_s).wait_send()
            ag_copy(l, g, peer(off), me_s).wait_send()
        later(lambda j: d_copy(l, g, j, me_d).wait_send())
        return c

    lax.fori_loop(0, LAYERS * groups, drain, 0)


def local(shards, spans, frames, cloud_mask, qkv_weight, out_weight, norm_gain, head_norm_scale, decay):
    dates, here, width = frames.shape
    tokens = dates * here
    groups = width // COLS
    rows = HEAD // shards
    wire = jnp.bfloat16 if rows % 16 == 0 else jnp.float32
    vmem = pl.BlockSpec(memory_space=pltpu.VMEM)
    hbm = pl.BlockSpec(memory_space=pl.ANY)
    bf16, f32 = jnp.bfloat16, jnp.float32
    block = (shards, dates * rows, COLS)
    dma = pltpu.SemaphoreType.DMA
    out = pl.pallas_call(
        functools.partial(kernel, shards, spans, dates),
        out_shape=jax.ShapeDtypeStruct((tokens, width), bf16),
        in_specs=[hbm, vmem, hbm, hbm, vmem, vmem, vmem],
        out_specs=vmem,
        scratch_shapes=[
            pltpu.VMEM((16, width), f32),
            pltpu.VMEM((LAYERS, 4 * groups, width, COLS), bf16),
            pltpu.VMEM((tokens, width), bf16),
            pltpu.VMEM((groups, tokens, COLS), bf16),
            pltpu.VMEM((tokens, width), bf16),
            pltpu.VMEM((tokens, COLS), f32),
            pltpu.VMEM((tokens, COLS), bf16),
            pltpu.VMEM((tokens, COLS), bf16),
            pltpu.VMEM((groups,) + block, f32),
            pltpu.VMEM((groups, dates * rows, COLS), f32),
            pltpu.VMEM((LAYERS, groups) + block, bf16),
            pltpu.VMEM((LAYERS, groups) + block, bf16),
            pltpu.VMEM((LAYERS, groups, rows, COLS), wire),
            pltpu.VMEM((LAYERS, groups, spans, rows, COLS), wire),
            pltpu.VMEM((LAYERS, groups) + block, bf16),
            pltpu.VMEM((spans, 8, width), f32),
            dma,
            dma((LAYERS, 4 * groups)),
            dma((LAYERS, groups, shards)),
            dma((LAYERS, groups, shards)),
            dma((LAYERS, groups, spans)),
            dma((LAYERS, groups, spans)),
            dma((LAYERS, groups, shards)),
            dma((LAYERS, groups, shards)),
            dma((spans,)),
            dma((spans,)),
        ],
        compiler_params=pltpu.CompilerParams(
            collective_id=0, has_side_effects=True, vmem_limit_bytes=56 * 2**20
        ),
    )(
        frames.reshape(tokens, width), cloud_mask, qkv_weight, out_weight,
        norm_gain, head_norm_scale, decay,
    )
    return out.reshape(frames.shape)


def solution(mesh):
    placed = (
        P("date", "space", None),
        P("date", "space"),
        P(),
        P(),
        P(),
        P(),
        P(None, "date", None),
    )
    return jax.shard_map(
        functools.partial(local, mesh.shape["space"], mesh.shape["date"]),
        mesh=mesh,
        in_specs=placed,
        out_specs=P("date", "space", None),
        check_vma=False,
    )
```

```python
import functools

import jax
import jax.numpy as jnp
from jax import lax
from jax.experimental import pallas as pl
from jax.experimental.pallas import tpu as pltpu
from jax.sharding import PartitionSpec as P

HEADS = 16
HEAD = 64
LAYERS = 2
COLS = 256
MESH = pl.DeviceIdType.MESH


def feature(u):
    return jnp.where(u > 0.0, u + 1.0, jnp.exp(jnp.minimum(u, 0.0)))


def kernel(
    shards, spans, dates,
    frames, mask, wqkv, wout, gain, hscale, decay, out,
    tbl, wbuf, nb, qb, mb, maskb, kb, vb, acc, part, own, lst, rs_send, rs_recv, y_send, y_recv, dsend, drecv, sb, tks,
    fsem, wsem, p_ss, p_rs, y_ss, y_rs, d_ss, d_rs, ag_ss, ag_rs, fw_ss, tk_ss, tk_rs,
):
    tokens, width = out.shape
    here = tokens // dates
    groups = width // COLS
    rows = HEAD // shards
    me_s, me_d = lax.axis_index("space"), lax.axis_index("date")

    lines, line, core = shards // 2, me_s // 2, lax.rem(me_s, 2)
    mate = me_s + 1 - 2 * core

    def across(off):
        return lax.rem(line + off, lines)

    barrier = pltpu.get_barrier_semaphore()
    pl.semaphore_signal(barrier, inc=1, device_id={"space": mate}, device_id_type=MESH)
    for off in range(1, lines):
        pl.semaphore_signal(
            barrier, inc=1, device_id={"space": 2 * across(off) + core}, device_id_type=MESH
        )
    for off in range(1, spans):
        pl.semaphore_signal(
            barrier, inc=1, device_id={"date": lax.rem(me_d + off, spans)}, device_id_type=MESH
        )

    def frame_copy():
        return pltpu.make_async_copy(frames, out, fsem)

    def qkv_copy(l, c):
        cols = pl.ds(pl.multiple_of(c * COLS, COLS), COLS)
        return pltpu.make_async_copy(wqkv.at[l, :, cols], wbuf.at[l, c], wsem.at[l, c])

    def out_copy(l, c):
        cols = pl.ds(pl.multiple_of(c * COLS, COLS), COLS)
        slot = c + 3 * groups
        return pltpu.make_async_copy(wout.at[l, :, cols], wbuf.at[l, slot], wsem.at[l, slot])

    frame_copy().start()
    for l in range(LAYERS):
        for g in range(groups):
            qkv_copy(l, groups + g).start()
            qkv_copy(l, 2 * groups + g).start()
        for g in range(groups):
            qkv_copy(l, g).start()
        for g in range(groups):
            out_copy(l, g).start()

    flags = mask[...].astype(jnp.float32)
    for t in range(dates):
        pick = lax.broadcasted_iota(jnp.int32, (dates, COLS), 0) == t
        maskb[pl.ds(t * here, here), :] = lax.dot_general(
            flags, jnp.where(pick, 1.0, 0.0), (((0,), (0,)), ((), ())),
            preferred_element_type=jnp.float32,
        )

    spread = jnp.where(
        lax.broadcasted_iota(jnp.int32, (HEADS, width), 1) // HEAD
        == lax.broadcasted_iota(jnp.int32, (HEADS, width), 0), 1.0, 0.0,
    )
    tail = []
    for l in range(LAYERS):
        kept_l = jnp.dot(
            decay[l], spread, precision=lax.Precision.HIGHEST, preferred_element_type=jnp.float32
        )
        tbl[pl.ds(l * dates, dates), :] = kept_l
        whole = kept_l[0:1, :]
        for t in range(1, dates):
            whole = whole * kept_l[t : t + 1, :]
        tail.append(whole)
    tbl[8:16, :] = jnp.concatenate(tail + [jnp.zeros((8 - LAYERS, width), jnp.float32)], 0)

    pl.semaphore_wait(barrier, lines + spans - 1)

    def tk_copy(j):
        return pltpu.make_async_remote_copy(
            src_ref=tbl.at[8:16], dst_ref=tks.at[me_d], send_sem=tk_ss.at[j],
            recv_sem=tk_rs.at[me_d], device_id={"date": j}, device_id_type=MESH,
        )

    def tk_arrival(j):
        return pltpu.make_async_remote_copy(
            src_ref=tbl.at[8:16], dst_ref=tks.at[j], send_sem=tk_ss.at[j],
            recv_sem=tk_rs.at[j], device_id={"date": j}, device_id_type=MESH,
        )

    def pair_copy(l, g):
        return pltpu.make_async_remote_copy(
            src_ref=rs_send.at[l, g], dst_ref=rs_recv.at[l, g],
            send_sem=p_ss.at[l, g], recv_sem=p_rs.at[l, g],
            device_id={"space": mate}, device_id_type=MESH,
        )

    def y_copy(l, g, y, slot):
        return pltpu.make_async_remote_copy(
            src_ref=y_send.at[l, g, y], dst_ref=y_recv.at[l, g, slot],
            send_sem=y_ss.at[l, g, y], recv_sem=y_rs.at[l, g, slot],
            device_id={"space": 2 * y + core}, device_id_type=MESH,
        )

    def fw_copy(l, g, slot):
        return pltpu.make_async_remote_copy(
            src_ref=sb.at[l, g, slot], dst_ref=sb.at[l, g, slot],
            send_sem=fw_ss.at[l, g, slot], recv_sem=ag_rs.at[l, g, slot],
            device_id={"space": mate}, device_id_type=MESH,
        )

    def d_copy(l, g, j, slot):
        return pltpu.make_async_remote_copy(
            src_ref=dsend.at[l, g], dst_ref=drecv.at[l, g, slot],
            send_sem=d_ss.at[l, g, j], recv_sem=d_rs.at[l, g, slot],
            device_id={"date": j}, device_id_type=MESH,
        )

    def ag_copy(l, g, p, slot):
        return pltpu.make_async_remote_copy(
            src_ref=sb.at[l, g, slot], dst_ref=sb.at[l, g, slot],
            send_sem=ag_ss.at[l, g, p], recv_sem=ag_rs.at[l, g, slot],
            device_id={"space": p}, device_id_type=MESH,
        )

    def later(f):
        def body(j, c):
            f(j)
            return c

        lax.fori_loop(me_d + 1, spans, body, 0)

    later(lambda j: tk_copy(j).start())
    frame_copy().wait()

    def columns(g):
        return pl.ds(pl.multiple_of(g * COLS, COLS), COLS)

    def by_layer(ref, l, first, second, cols):
        return jnp.where(l == 0, ref[first : first + 1, cols], ref[second : second + 1, cols])

    def norm(l):
        scale = jnp.where(l == 0, gain[0:1, :], gain[1:2, :])

        def body(t, c):
            at = pl.ds(pl.multiple_of(t * COLS, COLS), COLS)
            xf = out[at, :].astype(jnp.float32)
            msq = jnp.mean(xf * xf, -1, keepdims=True) + 1e-05
            nb[at, :] = (xf * lax.rsqrt(msq) * scale).astype(jnp.bfloat16)
            return c

        lax.fori_loop(0, tokens // COLS, body, 0)

    def keys(l, g):
        qkv_copy(l, groups + g).wait()
        qkv_copy(l, 2 * groups + g).wait()
        k = jnp.dot(nb[...], wbuf[l, groups + g], preferred_element_type=jnp.float32)
        kb[...] = (feature(k) * maskb[...]).astype(jnp.bfloat16)
        vb[...] = jnp.dot(
            nb[...], wbuf[l, 2 * groups + g], preferred_element_type=jnp.float32
        ).astype(jnp.bfloat16)
        head = lax.broadcasted_iota(jnp.int32, (HEAD, COLS), 1) // HEAD
        for t in range(dates):
            at = pl.ds(t * here, here)
            pair = lax.dot_general(
                kb[at, :], vb[at, :], (((0,), (0,)), ((), ())), preferred_element_type=jnp.float32
            )
            small = jnp.zeros((HEAD, COLS), jnp.float32)
            for h in range(COLS // HEAD):
                small = jnp.where(head == h, pair[h * HEAD : (h + 1) * HEAD, :], small)
            for r in range(shards):
                part[g, r % 2, r // 2, pl.ds(t * rows, rows), :] = small[r * rows : (r + 1) * rows, :]
        rs_send[l, g] = part[g, 1 - core].astype(jnp.bfloat16)
        pair_copy(l, g).start()

    def paired(l, g):
        pair_copy(l, g).wait_recv()
        for off in range(1, lines):
            y = across(off)
            y_send[l, g, y] = (part[g, core, y] + rs_recv[l, g, y].astype(jnp.float32)).astype(
                jnp.bfloat16
            )
            y_copy(l, g, y, line).start()
        own[g] = part[g, core, line] + rs_recv[l, g, line].astype(jnp.float32)

    def queries(l, g):
        qkv_copy(l, g).wait()
        q = jnp.dot(nb[...], wbuf[l, g], preferred_element_type=jnp.float32)
        qb[g] = feature(q).astype(jnp.bfloat16)

    def decays(l, g, t):
        return by_layer(tbl, l, t, dates + t, columns(g))

    def summed(l, g):
        total = own[g]
        for off in range(1, lines):
            y = across(off)
            y_copy(l, g, y, y).wait_recv()
            total = total + y_recv[l, g, y].astype(jnp.float32)
        state = jnp.zeros((rows, COLS), jnp.float32)
        for t in range(dates):
            state = decays(l, g, t) * state + total[t * rows : (t + 1) * rows, :]
            lst[g, pl.ds(t * rows, rows), :] = state
        dsend[l, g] = state.astype(dsend.dtype)
        later(lambda j: d_copy(l, g, j, me_d).start())

    def joined(l, g):
        @pl.when((l == 0) & (g == 0))
        def _():
            def arrive(j, c):
                tk_arrival(j).wait_recv()
                return c

            lax.fori_loop(0, me_d, arrive, 0)

        def earlier(j, carry):
            d_copy(l, g, j, j).wait_recv()
            kept = jnp.where(l == 0, tks[j, 0:1, columns(g)], tks[j, 1:2, columns(g)])
            return kept * carry + drecv[l, g, j].astype(jnp.float32)

        carry = lax.fori_loop(0, me_d, earlier, jnp.zeros((rows, COLS), jnp.float32))
        states = []
        for t in range(dates):
            carry = decays(l, g, t) * carry
            states.append(lst[g, pl.ds(t * rows, rows), :] + carry)
        sb[l, g, me_s] = jnp.concatenate(states, 0).astype(jnp.bfloat16)
        for off in range(1, lines):
            ag_copy(l, g, 2 * across(off) + core, me_s).start()
        ag_copy(l, g, mate, me_s).start()

    def forwarded(l, g):
        for off in range(1, lines):
            slot = 2 * across(off) + core
            ag_copy(l, g, slot, slot).wait_recv()
            fw_copy(l, g, slot).start()

    def mix(l, g):
        ag_copy(l, g, mate, mate).wait_recv()
        for off in range(1, lines):
            fw_copy(l, g, 2 * across(off) + 1 - core).wait_recv()
        blocks = [sb[l, g, r].astype(jnp.float32) for r in range(shards)]
        head = lax.broadcasted_iota(jnp.int32, (HEAD, COLS), 1) // HEAD
        wide = lax.broadcasted_iota(jnp.int32, (COLS, COLS), 1) // HEAD
        tall = lax.broadcasted_iota(jnp.int32, (COLS, COLS), 0) // HEAD
        ones = jnp.where(wide == tall, 1.0, 0.0).astype(jnp.bfloat16)
        scale = by_layer(hscale, l, 0, 1, columns(g))
        for t in range(dates):
            small = jnp.concatenate([b[t * rows : (t + 1) * rows, :] for b in blocks], 0)
            big = jnp.concatenate(
                [jnp.where(head == h, small, 0.0) for h in range(COLS // HEAD)], 0
            ).astype(jnp.bfloat16)
            numer = jnp.dot(
                qb[g, pl.ds(t * here, here), :], big, preferred_element_type=jnp.float32
            )
            msq = jnp.dot(
                (numer * numer).astype(jnp.bfloat16), ones, preferred_element_type=jnp.float32
            )
            msq = msq * (1.0 / HEAD) + 1e-05
            mb[pl.ds(t * here, here), columns(g)] = (numer * lax.rsqrt(msq) * scale).astype(
                jnp.bfloat16
            )

    half = width // 2

    def project_first(l, c):
        out_copy(l, c).wait()
        update = jnp.dot(
            mb[:, :half], wbuf[l, 3 * groups + c, :half], preferred_element_type=jnp.float32
        )
        acc[c] = out[:, columns(c)].astype(jnp.float32) + update

    def project_rest(l, c):
        update = jnp.dot(
            mb[:, half:], wbuf[l, 3 * groups + c, half:], preferred_element_type=jnp.float32
        )
        out[:, columns(c)] = (acc[c] + update).astype(jnp.bfloat16)

    def layer(l, c0):
        norm(l)

        def step(s, c):
            @pl.when(s < groups)
            def _():
                keys(l, s)

            @pl.when(s >= groups)
            def _():
                queries(l, s - groups)

            @pl.when((s >= 1) & (s < groups + 1))
            def _():
                paired(l, s - 1)

            @pl.when((s >= 2) & (s < groups + 2))
            def _():
                summed(l, s - 2)

            @pl.when(s >= groups)
            def _():
                joined(l, s - groups)

            @pl.when(s >= groups + 1)
            def _():
                forwarded(l, s - groups - 1)

            return c

        lax.fori_loop(0, 2 * groups, step, 0)

        def each(first, last, f):
            def body(i, c):
                f(l, i)
                return c

            lax.fori_loop(first, last, body, 0)

        each(0, groups // 2, mix)
        forwarded(l, groups - 1)
        each(0, groups, project_first)
        each(groups // 2, groups, mix)
        each(0, groups, project_rest)
        return c0

    lax.fori_loop(0, LAYERS, layer, 0)

    later(lambda j: tk_copy(j).wait_send())

    def drain(i, c):
        l, g = i // groups, lax.rem(i, groups)
        pair_copy(l, g).wait_send()
        ag_copy(l, g, mate, me_s).wait_send()
        for off in range(1, lines):
            y_copy(l, g, across(off), line).wait_send()
            ag_copy(l, g, 2 * across(off) + core, me_s).wait_send()
            fw_copy(l, g, 2 * across(off) + core).wait_send()
        later(lambda j: d_copy(l, g, j, me_d).wait_send())
        return c

    lax.fori_loop(0, LAYERS * groups, drain, 0)


def local(shards, spans, frames, cloud_mask, qkv_weight, out_weight, norm_gain, head_norm_scale, decay):
    dates, here, width = frames.shape
    tokens = dates * here
    groups = width // COLS
    rows = HEAD // shards
    wire = jnp.bfloat16 if rows % 16 == 0 else jnp.float32
    vmem = pl.BlockSpec(memory_space=pltpu.VMEM)
    hbm = pl.BlockSpec(memory_space=pl.ANY)
    bf16, f32 = jnp.bfloat16, jnp.float32
    block = (shards, dates * rows, COLS)
    split = (shards // 2, dates * rows, COLS)
    dma = pltpu.SemaphoreType.DMA
    out = pl.pallas_call(
        functools.partial(kernel, shards, spans, dates),
        out_shape=jax.ShapeDtypeStruct((tokens, width), bf16),
        in_specs=[hbm, vmem, hbm, hbm, vmem, vmem, vmem],
        out_specs=vmem,
        scratch_shapes=[
            pltpu.VMEM((16, width), f32),
            pltpu.VMEM((LAYERS, 4 * groups, width, COLS), bf16),
            pltpu.VMEM((tokens, width), bf16),
            pltpu.VMEM((groups, tokens, COLS), bf16),
            pltpu.VMEM((tokens, width), bf16),
            pltpu.VMEM((tokens, COLS), f32),
            pltpu.VMEM((tokens, COLS), bf16),
            pltpu.VMEM((tokens, COLS), bf16),
            pltpu.VMEM((groups, tokens, COLS), f32),
            pltpu.VMEM((groups, 2) + split, f32),
            pltpu.VMEM((groups, dates * rows, COLS), f32),
            pltpu.VMEM((groups, dates * rows, COLS), f32),
            pltpu.VMEM((LAYERS, groups) + split, bf16),
            pltpu.VMEM((LAYERS, groups) + split, bf16),
            pltpu.VMEM((LAYERS, groups) + split, bf16),
            pltpu.VMEM((LAYERS, groups) + split, bf16),
            pltpu.VMEM((LAYERS, groups, rows, COLS), wire),
            pltpu.VMEM((LAYERS, groups, spans, rows, COLS), wire),
            pltpu.VMEM((LAYERS, groups) + block, bf16),
            pltpu.VMEM((spans, 8, width), f32),
            dma,
            dma((LAYERS, 4 * groups)),
            dma((LAYERS, groups)),
            dma((LAYERS, groups)),
            dma((LAYERS, groups, shards // 2)),
            dma((LAYERS, groups, shards // 2)),
            dma((LAYERS, groups, spans)),
            dma((LAYERS, groups, spans)),
            dma((LAYERS, groups, shards)),
            dma((LAYERS, groups, shards)),
            dma((LAYERS, groups, shards)),
            dma((spans,)),
            dma((spans,)),
        ],
        compiler_params=pltpu.CompilerParams(
            collective_id=0, has_side_effects=True, vmem_limit_bytes=56 * 2**20
        ),
    )(
        frames.reshape(tokens, width), cloud_mask, qkv_weight, out_weight,
        norm_gain, head_norm_scale, decay,
    )
    return out.reshape(frames.shape)


def solution(mesh):
    placed = (
        P("date", "space", None),
        P("date", "space"),
        P(),
        P(),
        P(),
        P(),
        P(None, "date", None),
    )
    return jax.shard_map(
        functools.partial(local, mesh.shape["space"], mesh.shape["date"]),
        mesh=mesh,
        in_specs=placed,
        out_specs=P("date", "space", None),
        check_vma=False,
    )
```
